32 devices in a mesh: groups: 2 (over y), dp: 4 (over z), gy: 4 (over x, core).
Axes of the slice: x: 2, y: 2, z: 4, core: 2. Of those that a mesh axis runs over, the one named last changes fastest.
Arguments:
- fields: bfloat16 [8, 96, 32, 512], P(('groups', 'dp'), None, 'gy'), parts along dimension 0, may hold values from -6 to 6
- kernel_taps: bfloat16 [27, 96, 96], replicated, may hold values from -0.125 to 0.125
- bias_vector: float32 [96], replicated, may hold values from -4 to 4
- cotangent: bfloat16 [8, 96, 32, 512], P(('groups', 'dp'), None, 'gy'), parts along dimension 0, may hold values from -6 to 6
Outputs:
- activated: bfloat16 [8, 96, 32, 512], P(('groups', 'dp'), None, 'gy'), parts along dimension 0
- field_grad: bfloat16 [8, 96, 32, 512], P(('groups', 'dp'), None, 'gy'), parts along dimension 0
- kernel_grad: float32 [54, 96, 96], P('groups'), parts along dimension 0
- bias_grad: float32 [192], P('groups'), parts along dimension 0
The draws below stay inside these ranges and needn't reach their ends.
There are 2 independent parts, one for each index of `groups`. The reference program is written for one: setup_inputs(seed, part) draws one part's arguments, and reference() takes and returns one part's arrays. A program takes and returns all parts, laid end to end along the dimension named above; an argument that names none is the same for every part. Nothing has to cross between parts.
All inputs are finite; a program needn't handle non-finite values.
Results may differ from the reference program's by a relative error of at most 0.0049.
Values may be sent and summed in bfloat16 or wider, within the bound.
A program may use at most 64 MiB of HBM per device.

```python
import jax
import jax.numpy as jnp
from jax import lax

C = 96
TAPS = 27
CZ = 16
RUNS = 4
NY = 32
CELLS = 512


def steps_of(stream_key, extent, split, smallest, high):
    def one(position, shards_of):
        steps = jax.random.uniform(jax.random.fold_in(jax.random.fold_in(stream_key, 6), position), (shards_of,), jnp.float32, smallest / len(split), high / len(split))
        return jnp.repeat(jnp.exp(steps), extent[position] // shards_of).reshape((-1,) + (1,) * (len(extent) - position - 1))

    loudness = one(*split[0])
    for cut in split[1:]:
        loudness = loudness * one(*cut)
    return loudness


def centred(key, extent, scale, most, split=(), kind=jnp.bfloat16):
    values = jax.random.normal(key, extent, jnp.float32) * scale
    if len(split) > 0:
        values = steps_of(key, extent, split, -0.22, 0.18) * values
    return jnp.clip(values, min=-most, max=most).astype(kind)


def setup_inputs(seed: int = 0, part: int = 0) -> dict:
    key_of = jax.random.split(jax.random.key(seed), 5)
    part_keys = jax.random.split(jax.random.fold_in(key_of[4], part), 5)
    fields = centred(part_keys[0], (RUNS, C, NY, CELLS), 1.0, 6.0, ((0, 4), (2, 4)))
    kernel_taps = centred(key_of[1], (TAPS, C, C), (TAPS * C) ** -0.5, 0.125)
    bias_vector = centred(key_of[2], (C,), 1.0, 4.0, (), jnp.float32)
    cotangent = centred(part_keys[3], (RUNS, C, NY, CELLS), 1.0, 6.0, ((0, 4), (2, 4)))
    return dict(fields=fields, kernel_taps=kernel_taps, bias_vector=bias_vector, cotangent=cotangent)


clip_norm = 512.0

def shift_cells(values, step_x, step_z):
    cells = values.shape[-1]
    offset = step_x * CZ + step_z
    blank = jnp.zeros(values.shape[:-1] + (abs(offset),), values.dtype)
    if offset > 0:
        moved_cells = jnp.concatenate([values[..., offset:], blank], axis=-1)
    elif offset < 0:
        moved_cells = jnp.concatenate([blank, values[..., :cells + offset]], axis=-1)
    else:
        moved_cells = values
    depth = jnp.arange(cells) % CZ
    valid_cells = (depth + step_z >= 0) & (depth + step_z < CZ)
    return jnp.where(valid_cells, moved_cells, jnp.zeros((), values.dtype))

def tap_patches(padded, tap_y, tap_x, row_count, direction):
    first_row = 2 * tap_y if direction > 0 else 4 - 2 * tap_y
    window = padded[..., first_row:first_row + row_count, :]
    pieces = [shift_cells(window, direction * 2 * (tap_x - 1), direction * 2 * (tap_z - 1)) for tap_z in range(3)]
    return jnp.concatenate(pieces, axis=-3)

def weight_block(kernel_taps, tap_y, tap_x, direction):
    first_tap = 9 * tap_y + 3 * tap_x
    matrices = [kernel_taps[first_tap + tap_z] for tap_z in range(3)]
    if direction < 0:
        matrices = [one_tap.T for one_tap in matrices]
    return jnp.concatenate(matrices, axis=1)

def convolve(padded, kernel_taps, row_count, direction):
    accum = jnp.zeros((kernel_taps.shape[1], row_count, padded.shape[-1]), jnp.float32)
    for tap_y in range(3):
        for tap_x in range(3):
            patches = tap_patches(padded, tap_y, tap_x, row_count, direction).astype(jnp.float32)
            block = weight_block(kernel_taps, tap_y, tap_x, direction).astype(jnp.float32)
            accum = accum + jnp.einsum('ok,kyp->oyp', block, patches, precision=lax.Precision.HIGHEST)
    return accum

def kernel_grads(padded_in, slope, row_count):
    channels = slope.shape[0]
    results = []
    for tap_y in range(3):
        for tap_x in range(3):
            patches = tap_patches(padded_in, tap_y, tap_x, row_count, 1).astype(jnp.float32)
            grads = jnp.einsum('oyp,kyp->ok', slope.astype(jnp.float32), patches, precision=lax.Precision.HIGHEST)
            results.append(grads.reshape(channels, 3, channels).transpose(1, 0, 2))
    return jnp.concatenate(results, axis=0)

def reference(fields, kernel_taps, bias_vector, cotangent):

    def single_run(pair):
        fields_run, cot_run = pair
        row_count = fields_run.shape[1]
        padded_in = jnp.pad(fields_run, ((0, 0), (2, 2), (0, 0)))
        pre_act = convolve(padded_in, kernel_taps, row_count, 1) + bias_vector[:, None, None]
        activated = jax.nn.gelu(pre_act).astype(jnp.bfloat16)
        unused, pull_back = jax.vjp(jax.nn.gelu, pre_act)
        slope = pull_back(cot_run.astype(pre_act.dtype))[0].astype(jnp.bfloat16)
        padded_slope = jnp.pad(slope, ((0, 0), (2, 2), (0, 0)))
        field_grad = convolve(padded_slope, kernel_taps, row_count, -1).astype(jnp.bfloat16)
        run_kernel = kernel_grads(padded_in, slope, row_count)
        run_bias = lax.optimization_barrier(jnp.sum(slope.astype(jnp.float32), axis=(1, 2)))
        return (activated, field_grad, run_kernel, run_bias)
    activated, field_grad, run_kernels, run_biases = lax.map(single_run, (fields, cotangent))
    wsum = lax.optimization_barrier(jnp.sum(run_kernels, axis=0))
    bsum = lax.optimization_barrier(jnp.sum(run_biases, axis=0))
    grad_norm = jnp.sqrt(jnp.sum(wsum * wsum) + jnp.sum(bsum * bsum) + 1e-06)
    factor = jnp.minimum(1.0, clip_norm / grad_norm)
    return (activated, field_grad, wsum * factor, bsum * factor)
```

```python
import functools

import jax
import jax.numpy as jnp
from jax import lax
from jax.experimental import pallas as pl
from jax.experimental.pallas import tpu as pltpu
from jax.sharding import PartitionSpec as P

CZ = 16
clip_norm = 512.0
ROOT = 0.7978845608028654


def to_rows(src_ref, tile_ref, put):
    channels, count, cells = src_ref.shape
    for lane in range(cells // 128):
        part = src_ref[:, :, lane * 128 : lane * 128 + 128].astype(jnp.float32)
        tile_ref[lane, : channels * count, :] = part.reshape(channels * count, 128)
    for row in range(count):
        for lane in range(cells // 128):
            put(row, lane, tile_ref[lane, pl.ds(row, channels, stride=count), :])


def from_rows(dst_ref, tile_ref):
    channels, count, cells = dst_ref.shape
    for lane in range(cells // 128):
        part = tile_ref[lane, : channels * count, :].reshape(channels, count, 128)
        dst_ref[:, :, lane * 128 : lane * 128 + 128] = part.astype(dst_ref.dtype)


def build(row, patch_ref, index):
    channels, cells = row.shape
    place = lax.broadcasted_iota(jnp.int32, (1, cells), 1)
    depth = place % CZ
    wide = row.astype(jnp.float32)
    for tx in range(3):
        for tz in range(3):
            k = 3 * tx + tz
            dx, dz = 2 * (tx - 1), 2 * (tz - 1)
            offset = dx * CZ + dz
            if offset == 0:
                moved = row
            else:
                valid = (depth + dz >= 0) & (depth + dz < CZ)
                valid = valid & (place + dx * CZ >= 0) & (place + dx * CZ < cells)
                moved = pltpu.roll(wide, (-offset) % cells, 1)
                moved = jnp.where(valid, moved, 0.0).astype(jnp.bfloat16)
            patch_ref[index, k * channels : (k + 1) * channels, :] = moved


def convolve_row(weight_ref, patch_ref, acc_ref, padded, first, last):
    channels = acc_ref.shape[1]
    result = jnp.dot(
        weight_ref[first * channels : last * channels, :],
        patch_ref[padded],
        preferred_element_type=jnp.float32,
    )
    for ty in range(first, last):
        part = result[(ty - first) * channels : (ty - first + 1) * channels]
        yield ty, padded - 2 * ty, part


def taps_of(padded, count):
    return [ty for ty in range(3) if 0 <= padded - 2 * ty < count]


def convolve(weight_ref, patch_ref, acc_ref, order):
    count = acc_ref.shape[0]
    seen = set()
    for padded in order:
        tys = taps_of(padded, count)
        for ty, y, part in convolve_row(
            weight_ref, patch_ref, acc_ref, padded, tys[0], tys[-1] + 1
        ):
            if y in seen:
                acc_ref[y] += part
            else:
                acc_ref[y] = part
                seen.add(y)


def gelu_pair(v, upstream):
    square = v * v
    t = jnp.tanh(ROOT * (v + 0.044715 * (v * square)))
    half = 0.5 * (1.0 + t)
    inner = ROOT * (1.0 + 3 * 0.044715 * square)
    return v * half, upstream * (half + 0.5 * v * (1.0 - t * t) * inner)


def forward_kernel(
    f_ref, up_ref, down_ref, w_ref, b_ref, cot_ref, act_ref, s_ref, wg_ref, bs_ref,
    tile_ref, x_ref, patch_ref, acc_ref, cot_rows_ref,
):
    channels, count, cells = f_ref.shape

    def putter(ref, base):
        def put(row, lane, value):
            ref[base + row, :, lane * 128 : lane * 128 + 128] = value.astype(jnp.bfloat16)

        return put

    to_rows(f_ref, tile_ref, putter(x_ref, 2))
    to_rows(up_ref, tile_ref, putter(x_ref, 0))
    to_rows(down_ref, tile_ref, putter(x_ref, count + 2))
    to_rows(cot_ref, tile_ref, putter(cot_rows_ref, 0))
    for padded in range(count + 4):
        build(x_ref[padded], patch_ref, padded)
    convolve(w_ref, patch_ref, acc_ref, range(count + 4))
    bias = b_ref[...]
    total = jnp.zeros((channels, 128), jnp.float32)
    for y in range(count):
        for lane in range(cells // 128):
            cut = slice(lane * 128, lane * 128 + 128)
            act, slope = gelu_pair(
                acc_ref[y, :, cut] + bias, cot_rows_ref[y, :, cut].astype(jnp.float32)
            )
            slope = slope.astype(jnp.bfloat16)
            s_ref[y, :, cut] = slope
            total = total + slope.astype(jnp.float32)
            tile_ref[lane, pl.ds(y, channels, stride=count), :] = act
    from_rows(act_ref, tile_ref)
    bs_ref[...] = total
    wg_ref[...] = jnp.zeros_like(wg_ref)
    for padded in range(count + 4):
        tys = taps_of(padded, count)
        left = jnp.concatenate([s_ref[padded - 2 * ty] for ty in tys], axis=0)
        grads = lax.dot_general(
            left, patch_ref[padded], (((1,), (1,)), ((), ())),
            preferred_element_type=jnp.float32,
        )
        wg_ref[tys[0] * channels : (tys[-1] + 1) * channels, :] += grads


def backward_kernel(s_ref, up_ref, down_ref, w_ref, fg_ref, tile_ref, patch_ref, acc_ref):
    channels, count, cells = fg_ref.shape
    for padded in range(count + 4):
        if padded < 2:
            row = up_ref[padded]
        elif padded < count + 2:
            row = s_ref[padded - 2]
        else:
            row = down_ref[padded - count - 2]
        build(row, patch_ref, padded)
    convolve(w_ref, patch_ref, acc_ref, range(count + 4))
    for y in range(count):
        for lane in range(cells // 128):
            cut = slice(lane * 128, lane * 128 + 128)
            tile_ref[lane, pl.ds(y, channels, stride=count), :] = acc_ref[y, :, cut]
    from_rows(fg_ref, tile_ref)


def halo(first, last, axis):
    count = lax.axis_size(axis)
    up = [(i, (i + 1) % count) for i in range(count - 1)]
    down = [(j, i) for i, j in up]
    return lax.ppermute(last, axis, up), lax.ppermute(first, axis, down)


def shards(fields, kernel_taps, bias_vector, cotangent):
    channels, count, cells = fields.shape[1:]
    x, cot = fields[0], cotangent[0]
    up, down = halo(x[:, :2], x[:, count - 2 :], "gy")
    taps = kernel_taps.reshape(3, 9, channels, channels)
    w_fwd = taps.transpose(0, 2, 1, 3).reshape(3 * channels, 9 * channels)
    w_bwd = taps[::-1, ::-1].transpose(0, 3, 1, 2).reshape(3 * channels, 9 * channels)
    vmem = pl.BlockSpec(memory_space=pltpu.VMEM)
    params = pltpu.CompilerParams(vmem_limit_bytes=56 * 1024 * 1024)
    f32, b16 = jnp.float32, jnp.bfloat16
    tile = pltpu.VMEM((cells // 128, channels * count, 128), f32)
    patch = pltpu.VMEM((count + 4, 9 * channels, cells), b16)
    acc = pltpu.VMEM((count, channels, cells), f32)
    activated, slope, wg, bs = pl.pallas_call(
        forward_kernel,
        out_shape=(
            jax.ShapeDtypeStruct((channels, count, cells), b16),
            jax.ShapeDtypeStruct((count, channels, cells), b16),
            jax.ShapeDtypeStruct((3 * channels, 9 * channels), f32),
            jax.ShapeDtypeStruct((channels, 128), f32),
        ),
        in_specs=[vmem] * 6,
        out_specs=(vmem,) * 4,
        scratch_shapes=[
            tile,
            pltpu.VMEM((count + 4, channels, cells), b16),
            patch,
            acc,
            pltpu.VMEM((count, channels, cells), b16),
        ],
        compiler_params=params,
    )(x, up, down, w_fwd, bias_vector[:, None], cot)
    s_up, s_down = halo(slope[:2], slope[count - 2 :], "gy")
    wsum, bsum = lax.psum((wg, jnp.sum(bs, axis=1)), ("dp", "gy"))
    field_grad = pl.pallas_call(
        backward_kernel,
        out_shape=jax.ShapeDtypeStruct((channels, count, cells), b16),
        in_specs=[vmem] * 4,
        out_specs=vmem,
        scratch_shapes=[tile, patch, acc],
        compiler_params=params,
        cost_estimate=pl.CostEstimate(
            flops=2 * 27 * channels * channels * cells * count,
            bytes_accessed=3000000, transcendentals=0,
        ),
    )(slope, s_up, s_down, w_bwd)
    grad_norm = jnp.sqrt(jnp.sum(wsum * wsum) + jnp.sum(bsum * bsum) + 1e-06)
    factor = jnp.minimum(1.0, clip_norm / grad_norm)
    kernel_grad = (wsum * factor).reshape(3, channels, 9, channels).transpose(0, 2, 1, 3)
    return (
        activated[None],
        field_grad[None],
        kernel_grad.reshape(27, channels, channels),
        bsum * factor,
    )


def solution(mesh):
    in_specs = (
        P(("groups", "dp"), None, "gy", None),
        P(),
        P(),
        P(("groups", "dp"), None, "gy", None),
    )
    out_specs = (
        P(("groups", "dp"), None, "gy", None),
        P(("groups", "dp"), None, "gy", None),
        P("groups", None, None),
        P("groups"),
    )
    return jax.shard_map(shards, mesh=mesh, in_specs=in_specs, out_specs=out_specs, check_vma=False)
```

```python
import jax
import jax.numpy as jnp
from jax import lax
from jax.experimental import pallas as pl
from jax.experimental.pallas import tpu as pltpu
from jax.sharding import PartitionSpec as P

CZ = 16
clip_norm = 512.0
ROOT = 0.7978845608028654


def to_rows(src_ref, tile_ref, put):
    channels, count, cells = src_ref.shape
    for lane in range(cells // 128):
        part = src_ref[:, :, lane * 128 : lane * 128 + 128].astype(jnp.float32)
        tile_ref[lane, : channels * count, :] = part.reshape(channels * count, 128)
    for row in range(count):
        for lane in range(cells // 128):
            put(row, lane, tile_ref[lane, pl.ds(row, channels, stride=count), :])


def from_rows(dst_ref, tile_ref):
    channels, count, cells = dst_ref.shape
    for lane in range(cells // 128):
        part = tile_ref[lane, : channels * count, :].reshape(channels, count, 128)
        dst_ref[:, :, lane * 128 : lane * 128 + 128] = part.astype(dst_ref.dtype)


def build(row, patch_ref, index):
    channels, cells = row.shape
    place = lax.broadcasted_iota(jnp.int32, (1, cells), 1)
    depth = place % CZ
    wide = row.astype(jnp.float32)
    for tx in range(3):
        for tz in range(3):
            k = 3 * tx + tz
            dx, dz = 2 * (tx - 1), 2 * (tz - 1)
            offset = dx * CZ + dz
            if offset == 0:
                moved = row
            else:
                valid = (depth + dz >= 0) & (depth + dz < CZ)
                valid = valid & (place + dx * CZ >= 0) & (place + dx * CZ < cells)
                moved = pltpu.roll(wide, (-offset) % cells, 1)
                moved = jnp.where(valid, moved, 0.0).astype(jnp.bfloat16)
            patch_ref[index, k * channels : (k + 1) * channels, :] = moved


def convolve_row(weight_ref, patch_ref, acc_ref, padded, first, last):
    channels = acc_ref.shape[1]
    result = jnp.dot(
        weight_ref[first * channels : last * channels, :],
        patch_ref[padded],
        preferred_element_type=jnp.float32,
    )
    for ty in range(first, last):
        part = result[(ty - first) * channels : (ty - first + 1) * channels]
        yield ty, padded - 2 * ty, part


def taps_of(padded, count):
    return [ty for ty in range(3) if 0 <= padded - 2 * ty < count]


def convolve(weight_ref, patch_ref, acc_ref, order, seen):
    count = acc_ref.shape[0]
    for padded in order:
        tys = taps_of(padded, count)
        for ty, y, part in convolve_row(
            weight_ref, patch_ref, acc_ref, padded, tys[0], tys[-1] + 1
        ):
            if y in seen:
                acc_ref[y] += part
            else:
                acc_ref[y] = part
                seen.add(y)


def gelu_pair(v, upstream):
    square = v * v
    t = jnp.tanh(ROOT * (v + 0.044715 * (v * square)))
    half = 0.5 * (1.0 + t)
    inner = ROOT * (1.0 + 3 * 0.044715 * square)
    return v * half, upstream * (half + 0.5 * v * (1.0 - t * t) * inner)


MESH = pl.DeviceIdType.MESH


def greet(axis):
    me, size = lax.axis_index(axis), lax.axis_size(axis)
    barrier = pltpu.get_barrier_semaphore()
    for peer in (lax.rem(me + size - 1, size), lax.rem(me + 1, size)):
        pl.semaphore_signal(barrier, inc=1, device_id={axis: peer}, device_id_type=MESH)
    pl.semaphore_wait(barrier, 2)


def halo(axis, first, last, before, after, sems):
    me, size = lax.axis_index(axis), lax.axis_size(axis)

    def up():
        return pltpu.make_async_remote_copy(
            src_ref=last, dst_ref=before, send_sem=sems.at[0], recv_sem=sems.at[1],
            device_id={axis: lax.rem(me + 1, size)}, device_id_type=MESH,
        )

    def down():
        return pltpu.make_async_remote_copy(
            src_ref=first, dst_ref=after, send_sem=sems.at[2], recv_sem=sems.at[3],
            device_id={axis: lax.rem(me + size - 1, size)}, device_id_type=MESH,
        )

    def start():
        @pl.when(me < size - 1)
        def _():
            up().start()

        @pl.when(me > 0)
        def _():
            down().start()

    def finish():
        @pl.when(me > 0)
        def _():
            up().wait_recv()
            down().wait_send()

        @pl.when(me == 0)
        def _():
            before[...] = jnp.zeros(before.shape, before.dtype)

        @pl.when(me < size - 1)
        def _():
            down().wait_recv()
            up().wait_send()

        @pl.when(me == size - 1)
        def _():
            after[...] = jnp.zeros(after.shape, after.dtype)

    return start, finish


def forward_kernel(
    f_ref, w_ref, b_ref, cot_ref, act_ref, s_ref, sums_ref,
    tile_ref, x_ref, before_ref, after_ref, patch_ref, acc_ref, cot_rows_ref, wg_ref, sems,
):
    channels, count, cells = f_ref.shape

    def putter(ref):
        def put(row, lane, value):
            ref[row, :, lane * 128 : lane * 128 + 128] = value.astype(jnp.bfloat16)

        return put

    greet("gy")
    to_rows(f_ref, tile_ref, putter(x_ref))
    start, finish = halo(
        "gy", x_ref.at[pl.ds(0, 2)], x_ref.at[pl.ds(count - 2, 2)], before_ref, after_ref, sems
    )
    start()
    to_rows(cot_ref, tile_ref, putter(cot_rows_ref))
    seen = set()
    for padded in range(2, count + 2):
        build(x_ref[padded - 2], patch_ref, padded)
    convolve(w_ref, patch_ref, acc_ref, range(2, count + 2), seen)
    finish()
    for row in range(2):
        build(before_ref[row], patch_ref, row)
        build(after_ref[row], patch_ref, count + 2 + row)
    convolve(w_ref, patch_ref, acc_ref, (0, 1, count + 2, count + 3), seen)
    bias = b_ref[...]
    total = jnp.zeros((channels, 128), jnp.float32)
    for y in range(count):
        for lane in range(cells // 128):
            cut = slice(lane * 128, lane * 128 + 128)
            act, slope = gelu_pair(
                acc_ref[y, :, cut] + bias, cot_rows_ref[y, :, cut].astype(jnp.float32)
            )
            slope = slope.astype(jnp.bfloat16)
            s_ref[y, :, cut] = slope
            total = total + slope.astype(jnp.float32)
            tile_ref[lane, pl.ds(y, channels, stride=count), :] = act
    from_rows(act_ref, tile_ref)
    wg_ref[...] = jnp.zeros_like(wg_ref)
    for padded in range(count + 4):
        tys = taps_of(padded, count)
        left = jnp.concatenate([s_ref[padded - 2 * ty] for ty in tys], axis=0)
        grads = lax.dot_general(
            left, patch_ref[padded], (((1,), (1,)), ((), ())),
            preferred_element_type=jnp.float32,
        )
        wg_ref[tys[0] * channels : (tys[-1] + 1) * channels, : 9 * channels] += grads
    height = 3 * channels
    for lane in range(wg_ref.shape[1] // 128):
        sums_ref[lane * height : (lane + 1) * height, :] = wg_ref[
            :, lane * 128 : lane * 128 + 128
        ].astype(jnp.bfloat16)
    square = jnp.concatenate([total, jnp.zeros((128 - channels, 128), jnp.float32)], axis=0)
    bias_row = jnp.sum(square.T, axis=0, keepdims=True)
    high = bias_row.astype(jnp.bfloat16).astype(jnp.float32)
    used = wg_ref.shape[1] // 128 * height
    index = lax.broadcasted_iota(jnp.int32, (sums_ref.shape[0] - used, 128), 0)
    rest = jnp.where(index == 0, high, jnp.where(index == 1, bias_row - high, 0.0))
    sums_ref[used:, :] = rest.astype(jnp.bfloat16)


def backward_kernel(
    s_ref, w_ref, sums_ref, fg_ref, kg_ref, bg_ref,
    tile_ref, patch_ref, acc_ref, before_ref, after_ref, land1_ref, land2_ref, part_ref, red_ref,
    sems, sends, recvs,
):
    channels, count, cells = fg_ref.shape
    outer, inner = lax.axis_size("gy"), lax.axis_size("dp")
    me_out, me_in = lax.axis_index("gy"), lax.axis_index("dp")
    rows1 = sums_ref.shape[0] // outer
    rows2 = rows1 // inner
    barrier = pltpu.get_barrier_semaphore()
    for axis, me, size in (("gy", me_out, outer), ("dp", me_in, inner)):
        for k in range(1, size):
            pl.semaphore_signal(
                barrier, inc=1, device_id={axis: lax.rem(me + k, size)}, device_id_type=MESH
            )
    pl.semaphore_wait(barrier, outer + inner - 2)

    def spread(axis, me, size, base, source, target):
        copies = []
        for k in range(1, size):
            peer = lax.rem(me + k, size)
            copies.append(
                pltpu.make_async_remote_copy(
                    src_ref=source(peer), dst_ref=target(k),
                    send_sem=sends.at[base + k], recv_sem=recvs.at[base + k],
                    device_id={axis: peer}, device_id_type=MESH,
                )
            )
        for copy in copies:
            copy.start()
        return copies

    def piece(ref, index, length):
        return ref.at[pl.ds(pl.multiple_of(index * length, length), length)]

    start, finish = halo(
        "gy", s_ref.at[pl.ds(0, 2)], s_ref.at[pl.ds(count - 2, 2)], before_ref, after_ref, sems
    )
    start()
    first = spread(
        "gy", me_out, outer, 0,
        lambda peer: piece(sums_ref, peer, rows1), lambda k: land1_ref.at[k - 1],
    )
    for padded in range(2, count + 2):
        build(s_ref[padded - 2], patch_ref, padded)
    seen = set()
    convolve(w_ref, patch_ref, acc_ref, range(2, count + 2), seen)
    for copy in first:
        copy.wait()
    total = piece(sums_ref, me_out, rows1)[...].astype(jnp.float32)
    for k in range(outer - 1):
        total = total + land1_ref[k].astype(jnp.float32)
    part_ref[...] = total.astype(jnp.bfloat16)
    second = spread(
        "dp", me_in, inner, outer,
        lambda peer: piece(part_ref, peer, rows2), lambda k: land2_ref.at[k - 1],
    )
    finish()
    for row in range(2):
        build(before_ref[row], patch_ref, row)
        build(after_ref[row], patch_ref, count + 2 + row)
    for copy in second:
        copy.wait()
    total = piece(part_ref, me_in, rows2)[...].astype(jnp.float32)
    for k in range(inner - 1):
        total = total + land2_ref[k].astype(jnp.float32)
    mine = piece(red_ref, me_out * inner + me_in, rows2)
    mine[...] = total.astype(jnp.bfloat16)
    third = spread("dp", me_in, inner, outer + inner, lambda peer: mine, lambda k: mine)
    convolve(w_ref, patch_ref, acc_ref, (0, 1, count + 2, count + 3), seen)
    for copy in third:
        copy.wait()
    block = piece(red_ref, me_out, rows1)
    fourth = spread("gy", me_out, outer, outer + 2 * inner, lambda peer: block, lambda k: block)
    for y in range(count):
        for lane in range(cells // 128):
            cut = slice(lane * 128, lane * 128 + 128)
            tile_ref[lane, pl.ds(y, channels, stride=count), :] = acc_ref[y, :, cut]
    from_rows(fg_ref, tile_ref)
    for copy in fourth:
        copy.wait()
    height = 3 * channels
    lanes = -(-9 * channels // 128)
    squares = jnp.zeros((height, 128), jnp.float32)
    for lane in range(lanes):
        value = red_ref[lane * height : (lane + 1) * height, :].astype(jnp.float32)
        squares = squares + value * value
    rest = red_ref[lanes * height : lanes * height + 32, :].astype(jnp.float32)
    bias_row = jnp.sum(rest, axis=0, keepdims=True)
    norm = jnp.sum(squares, axis=0, keepdims=True) + bias_row * bias_row
    norm = jnp.sqrt(jnp.sum(norm, axis=1, keepdims=True) + 1e-06)
    factor = jnp.minimum(1.0, clip_norm / norm)
    bg_ref[...] = bias_row * factor
    for ty in range(3):
        wide = jnp.concatenate(
            [
                red_ref[lane * height + ty * channels : lane * height + (ty + 1) * channels, :]
                .astype(jnp.float32)
                for lane in range(lanes)
            ],
            axis=1,
        ) * factor
        for k in range(9):
            kg_ref[9 * ty + k] = wide[:, k * channels : (k + 1) * channels]


def shards(fields, kernel_taps, bias_vector, cotangent):
    channels, count, cells = fields.shape[1:]
    x, cot = fields[0], cotangent[0]
    outer, inner = lax.axis_size("gy"), lax.axis_size("dp")
    taps = kernel_taps.reshape(3, 9, channels, channels)
    w_fwd = taps.transpose(0, 2, 1, 3).reshape(3 * channels, 9 * channels)
    w_bwd = taps[::-1, ::-1].transpose(0, 3, 1, 2).reshape(3 * channels, 9 * channels)
    vmem = pl.BlockSpec(memory_space=pltpu.VMEM)
    f32, b16 = jnp.float32, jnp.bfloat16
    tile = pltpu.VMEM((cells // 128, channels * count, 128), f32)
    patch = pltpu.VMEM((count + 4, 9 * channels, cells), b16)
    acc = pltpu.VMEM((count, channels, cells), f32)
    rows = pltpu.VMEM((count, channels, cells), b16)
    edge = pltpu.VMEM((2, channels, cells), b16)
    lanes = -(-9 * channels // 128)
    unit = 16 * outer * inner
    length = -(-(lanes * 3 * channels + 32) // unit) * unit
    rows1 = length // outer
    rows2 = rows1 // inner
    flops = 2 * 27 * channels * channels * cells * count

    def params(number):
        return pltpu.CompilerParams(
            vmem_limit_bytes=56 * 1024 * 1024, collective_id=number, has_side_effects=True
        )

    activated, slope, sums = pl.pallas_call(
        forward_kernel,
        out_shape=(
            jax.ShapeDtypeStruct((channels, count, cells), b16),
            jax.ShapeDtypeStruct((count, channels, cells), b16),
            jax.ShapeDtypeStruct((length, 128), b16),
        ),
        in_specs=[vmem] * 4,
        out_specs=(vmem,) * 3,
        scratch_shapes=[
            tile, rows, edge, edge, patch, acc, rows,
            pltpu.VMEM((3 * channels, lanes * 128), f32),
            pltpu.SemaphoreType.DMA((4,)),
        ],
        compiler_params=params(0),
        cost_estimate=pl.CostEstimate(
            flops=2 * flops, bytes_accessed=4000000, transcendentals=0
        ),
    )(x, w_fwd, bias_vector[:, None], cot)
    field_grad, kernel_grad, bias_row = pl.pallas_call(
        backward_kernel,
        out_shape=(
            jax.ShapeDtypeStruct((channels, count, cells), b16),
            jax.ShapeDtypeStruct((27, channels, channels), f32),
            jax.ShapeDtypeStruct((1, 128), f32),
        ),
        in_specs=[vmem] * 3,
        out_specs=(vmem,) * 3,
        scratch_shapes=[
            tile, patch, acc, edge, edge,
            pltpu.VMEM((outer - 1, rows1, 128), b16),
            pltpu.VMEM((inner - 1, rows2, 128), b16),
            pltpu.VMEM((rows1, 128), b16),
            pltpu.VMEM((length, 128), b16),
            pltpu.SemaphoreType.DMA((4,)),
            pltpu.SemaphoreType.DMA((2 * (outer + inner),)),
            pltpu.SemaphoreType.DMA((2 * (outer + inner),)),
        ],
        compiler_params=params(1),
        cost_estimate=pl.CostEstimate(flops=flops, bytes_accessed=4000000, transcendentals=0),
    )(slope, w_bwd, sums)
    return activated[None], field_grad[None], kernel_grad, bias_row[0, :channels]


def solution(mesh):
    in_specs = (
        P(("groups", "dp"), None, "gy", None),
        P(),
        P(),
        P(("groups", "dp"), None, "gy", None),
    )
    out_specs = (
        P(("groups", "dp"), None, "gy", None),
        P(("groups", "dp"), None, "gy", None),
        P("groups", None, None),
        P("groups"),
    )
    return jax.shard_map(shards, mesh=mesh, in_specs=in_specs, out_specs=out_specs, check_vma=False)
```

```python
import jax
import jax.numpy as jnp
from jax import lax
from jax.experimental import pallas as pl
from jax.experimental.pallas import tpu as pltpu
from jax.sharding import PartitionSpec as P

CZ = 16
clip_norm = 512.0
ROOT = 0.7978845608028654


def to_rows(src_ref, tile_ref, put):
    channels, count, cells = src_ref.shape
    for lane in range(cells // 128):
        part = src_ref[:, :, lane * 128 : lane * 128 + 128].astype(jnp.float32)
        tile_ref[lane, : channels * count, :] = part.reshape(channels * count, 128)
    for row in range(count):
        for lane in range(cells // 128):
            put(row, lane, tile_ref[lane, pl.ds(row, channels, stride=count), :])


def from_rows(dst_ref, tile_ref):
    channels, count, cells = dst_ref.shape
    for lane in range(cells // 128):
        part = tile_ref[lane, : channels * count, :].reshape(channels, count, 128)
        dst_ref[:, :, lane * 128 : lane * 128 + 128] = part.astype(dst_ref.dtype)


def build(row, patch_ref, index):
    channels, cells = row.shape
    place = lax.broadcasted_iota(jnp.int32, (1, cells), 1)
    depth = place % CZ
    wide = row.astype(jnp.float32)
    for tx in range(3):
        for tz in range(3):
            k = 3 * tx + tz
            dx, dz = 2 * (tx - 1), 2 * (tz - 1)
            offset = dx * CZ + dz
            if offset == 0:
                moved = row
            else:
                valid = (depth + dz >= 0) & (depth + dz < CZ)
                valid = valid & (place + dx * CZ >= 0) & (place + dx * CZ < cells)
                moved = pltpu.roll(wide, (-offset) % cells, 1)
                moved = jnp.where(valid, moved, 0.0).astype(jnp.bfloat16)
            patch_ref[index, k * channels : (k + 1) * channels, :] = moved


def convolve_row(weight_ref, patch_ref, acc_ref, padded, first, last):
    channels = acc_ref.shape[1]
    result = jnp.dot(
        weight_ref[first * channels : last * channels, :],
        patch_ref[padded],
        preferred_element_type=jnp.float32,
    )
    for ty in range(first, last):
        part = result[(ty - first) * channels : (ty - first + 1) * channels]
        yield ty, padded - 2 * ty, part


def taps_of(padded, count):
    return [ty for ty in range(3) if 0 <= padded - 2 * ty < count]


def convolve(weight_ref, patch_ref, acc_ref, order, seen):
    count = acc_ref.shape[0]
    for padded in order:
        tys = taps_of(padded, count)
        for ty, y, part in convolve_row(
            weight_ref, patch_ref, acc_ref, padded, tys[0], tys[-1] + 1
        ):
            if y in seen:
                acc_ref[y] += part
            else:
                acc_ref[y] = part
                seen.add(y)


def gelu_pair(v, upstream):
    square = v * v
    t = jnp.tanh(ROOT * (v + 0.044715 * (v * square)))
    half = 0.5 * (1.0 + t)
    inner = ROOT * (1.0 + 3 * 0.044715 * square)
    return v * half, upstream * (half + 0.5 * v * (1.0 - t * t) * inner)


MESH = pl.DeviceIdType.MESH


def greet(axis):
    me, size = lax.axis_index(axis), lax.axis_size(axis)
    barrier = pltpu.get_barrier_semaphore()
    for peer in (lax.rem(me + size - 1, size), lax.rem(me + 1, size)):
        pl.semaphore_signal(barrier, inc=1, device_id={axis: peer}, device_id_type=MESH)
    pl.semaphore_wait(barrier, 2)


def halo(axis, first, last, before, after, sems):
    me, size = lax.axis_index(axis), lax.axis_size(axis)

    def up():
        return pltpu.make_async_remote_copy(
            src_ref=last, dst_ref=before, send_sem=sems.at[0], recv_sem=sems.at[1],
            device_id={axis: lax.rem(me + 1, size)}, device_id_type=MESH,
        )

    def down():
        return pltpu.make_async_remote_copy(
            src_ref=first, dst_ref=after, send_sem=sems.at[2], recv_sem=sems.at[3],
            device_id={axis: lax.rem(me + size - 1, size)}, device_id_type=MESH,
        )

    def start():
        @pl.when(me < size - 1)
        def _():
            up().start()

        @pl.when(me > 0)
        def _():
            down().start()

    def finish():
        @pl.when(me > 0)
        def _():
            up().wait_recv()
            down().wait_send()

        @pl.when(me == 0)
        def _():
            before[...] = jnp.zeros(before.shape, before.dtype)

        @pl.when(me < size - 1)
        def _():
            down().wait_recv()
            up().wait_send()

        @pl.when(me == size - 1)
        def _():
            after[...] = jnp.zeros(after.shape, after.dtype)

    return start, finish


def forward_kernel(
    f_ref, taps_ref, b_ref, cot_ref, act_ref, s_ref, sums_ref,
    w_ref, tile_ref, x_ref, before_ref, after_ref, patch_ref, acc_ref, cot_rows_ref, wg_ref, sems,
):
    channels, count, cells = f_ref.shape

    def putter(ref):
        def put(row, lane, value):
            ref[row, :, lane * 128 : lane * 128 + 128] = value.astype(jnp.bfloat16)

        return put

    greet("gy")
    to_rows(f_ref, tile_ref, putter(x_ref))
    start, finish = halo(
        "gy", x_ref.at[pl.ds(0, 2)], x_ref.at[pl.ds(count - 2, 2)], before_ref, after_ref, sems
    )
    start()
    for ty in range(3):
        for k in range(9):
            w_ref[
                ty * channels : (ty + 1) * channels, k * channels : (k + 1) * channels
            ] = taps_ref[9 * ty + k]
    to_rows(cot_ref, tile_ref, putter(cot_rows_ref))
    seen = set()
    for padded in range(2, count + 2):
        build(x_ref[padded - 2], patch_ref, padded)
    convolve(w_ref, patch_ref, acc_ref, range(2, count + 2), seen)
    finish()
    for row in range(2):
        build(before_ref[row], patch_ref, row)
        build(after_ref[row], patch_ref, count + 2 + row)
    convolve(w_ref, patch_ref, acc_ref, (0, 1, count + 2, count + 3), seen)
    bias = jnp.broadcast_to(b_ref[...], (channels, channels)).T[:, :1]
    total = jnp.zeros((channels, 128), jnp.float32)
    for y in range(count):
        for lane in range(cells // 128):
            cut = slice(lane * 128, lane * 128 + 128)
            act, slope = gelu_pair(
                acc_ref[y, :, cut] + bias, cot_rows_ref[y, :, cut].astype(jnp.float32)
            )
            slope = slope.astype(jnp.bfloat16)
            s_ref[y, :, cut] = slope
            total = total + slope.astype(jnp.float32)
            tile_ref[lane, pl.ds(y, channels, stride=count), :] = act
    from_rows(act_ref, tile_ref)
    wg_ref[...] = jnp.zeros_like(wg_ref)
    for padded in range(count + 4):
        tys = taps_of(padded, count)
        left = jnp.concatenate([s_ref[padded - 2 * ty] for ty in tys], axis=0)
        grads = lax.dot_general(
            left, patch_ref[padded], (((1,), (1,)), ((), ())),
            preferred_element_type=jnp.float32,
        )
        wg_ref[tys[0] * channels : (tys[-1] + 1) * channels, : 9 * channels] += grads
    height = 3 * channels
    for lane in range(wg_ref.shape[1] // 128):
        sums_ref[lane * height : (lane + 1) * height, :] = wg_ref[
            :, lane * 128 : lane * 128 + 128
        ].astype(jnp.bfloat16)
    square = jnp.concatenate([total, jnp.zeros((128 - channels, 128), jnp.float32)], axis=0)
    bias_row = jnp.sum(square.T, axis=0, keepdims=True)
    high = bias_row.astype(jnp.bfloat16).astype(jnp.float32)
    used = wg_ref.shape[1] // 128 * height
    index = lax.broadcasted_iota(jnp.int32, (sums_ref.shape[0] - used, 128), 0)
    rest = jnp.where(index == 0, high, jnp.where(index == 1, bias_row - high, 0.0))
    sums_ref[used:, :] = rest.astype(jnp.bfloat16)


def backward_kernel(
    s_ref, taps_ref, sums_ref, fg_ref, kg_ref, bg_ref,
    w_ref, tile_ref, patch_ref, acc_ref, before_ref, after_ref, land1_ref, land2_ref, part_ref, red_ref,
    sems, sends, recvs,
):
    channels, count, cells = fg_ref.shape
    outer, inner = lax.axis_size("gy"), lax.axis_size("dp")
    me_out, me_in = lax.axis_index("gy"), lax.axis_index("dp")
    rows1 = sums_ref.shape[0] // outer
    rows2 = rows1 // inner
    barrier = pltpu.get_barrier_semaphore()
    for axis, me, size in (("gy", me_out, outer), ("dp", me_in, inner)):
        for k in range(1, size):
            pl.semaphore_signal(
                barrier, inc=1, device_id={axis: lax.rem(me + k, size)}, device_id_type=MESH
            )
    pl.semaphore_wait(barrier, outer + inner - 2)

    def spread(axis, me, size, base, source, target):
        copies = []
        for k in range(1, size):
            peer = lax.rem(me + k, size)
            copies.append(
                pltpu.make_async_remote_copy(
                    src_ref=source(peer), dst_ref=target(k),
                    send_sem=sends.at[base + k], recv_sem=recvs.at[base + k],
                    device_id={axis: peer}, device_id_type=MESH,
                )
            )
        for copy in copies:
            copy.start()
        return copies

    def piece(ref, index, length):
        return ref.at[pl.ds(pl.multiple_of(index * length, length), length)]

    start, finish = halo(
        "gy", s_ref.at[pl.ds(0, 2)], s_ref.at[pl.ds(count - 2, 2)], before_ref, after_ref, sems
    )
    start()
    first = spread(
        "gy", me_out, outer, 0,
        lambda peer: piece(sums_ref, peer, rows1), lambda k: land1_ref.at[k - 1],
    )
    for ty in range(3):
        for k in range(9):
            w_ref[
                ty * channels : (ty + 1) * channels, k * channels : (k + 1) * channels
            ] = taps_ref[26 - 9 * ty - k].astype(jnp.float32).T.astype(jnp.bfloat16)
    for padded in range(2, count + 2):
        build(s_ref[padded - 2], patch_ref, padded)
    seen = set()
    convolve(w_ref, patch_ref, acc_ref, range(2, count + 2), seen)
    for copy in first:
        copy.wait()
    total = piece(sums_ref, me_out, rows1)[...].astype(jnp.float32)
    for k in range(outer - 1):
        total = total + land1_ref[k].astype(jnp.float32)
    part_ref[...] = total.astype(jnp.bfloat16)
    second = spread(
        "dp", me_in, inner, outer,
        lambda peer: piece(part_ref, peer, rows2), lambda k: land2_ref.at[k - 1],
    )
    finish()
    for row in range(2):
        build(before_ref[row], patch_ref, row)
        build(after_ref[row], patch_ref, count + 2 + row)
    for copy in second:
        copy.wait()
    total = piece(part_ref, me_in, rows2)[...].astype(jnp.float32)
    for k in range(inner - 1):
        total = total + land2_ref[k].astype(jnp.float32)
    mine = piece(red_ref, me_out * inner + me_in, rows2)
    mine[...] = total.astype(jnp.bfloat16)
    third = spread("dp", me_in, inner, outer + inner, lambda peer: mine, lambda k: mine)
    convolve(w_ref, patch_ref, acc_ref, (0, 1, count + 2, count + 3), seen)
    for copy in third:
        copy.wait()
    block = piece(red_ref, me_out, rows1)
    fourth = spread("gy", me_out, outer, outer + 2 * inner, lambda peer: block, lambda k: block)
    for y in range(count):
        for lane in range(cells // 128):
            cut = slice(lane * 128, lane * 128 + 128)
            tile_ref[lane, pl.ds(y, channels, stride=count), :] = acc_ref[y, :, cut]
    from_rows(fg_ref, tile_ref)
    for copy in fourth:
        copy.wait()
    height = 3 * channels
    lanes = -(-9 * channels // 128)
    squares = jnp.zeros((height, 128), jnp.float32)
    for lane in range(lanes):
        value = red_ref[lane * height : (lane + 1) * height, :].astype(jnp.float32)
        squares = squares + value * value
    rest = red_ref[lanes * height : lanes * height + 32, :].astype(jnp.float32)
    bias_row = jnp.sum(rest, axis=0, keepdims=True)
    norm = jnp.sum(squares, axis=0, keepdims=True) + bias_row * bias_row
    norm = jnp.sqrt(jnp.sum(norm, axis=1, keepdims=True) + 1e-06)
    factor = jnp.minimum(1.0, clip_norm / norm)
    bg_ref[...] = bias_row * factor
    for ty in range(3):
        wide = jnp.concatenate(
            [
                red_ref[lane * height + ty * channels : lane * height + (ty + 1) * channels, :]
                .astype(jnp.float32)
                for lane in range(lanes)
            ],
            axis=1,
        ) * factor
        for k in range(9):
            kg_ref[9 * ty + k] = wide[:, k * channels : (k + 1) * channels]


def shards(fields, kernel_taps, bias_vector, cotangent):
    channels, count, cells = fields.shape[1:]
    x, cot = fields[0], cotangent[0]
    outer, inner = lax.axis_size("gy"), lax.axis_size("dp")
    vmem = pl.BlockSpec(memory_space=pltpu.VMEM)
    f32, b16 = jnp.float32, jnp.bfloat16
    tile = pltpu.VMEM((cells // 128, channels * count, 128), f32)
    patch = pltpu.VMEM((count + 4, 9 * channels, cells), b16)
    acc = pltpu.VMEM((count, channels, cells), f32)
    rows = pltpu.VMEM((count, channels, cells), b16)
    stack = pltpu.VMEM((3 * channels, 9 * channels), b16)
    edge = pltpu.VMEM((2, channels, cells), b16)
    lanes = -(-9 * channels // 128)
    unit = 16 * outer * inner
    length = -(-(lanes * 3 * channels + 32) // unit) * unit
    rows1 = length // outer
    rows2 = rows1 // inner
    flops = 2 * 27 * channels * channels * cells * count

    def params(number):
        return pltpu.CompilerParams(
            vmem_limit_bytes=56 * 1024 * 1024, collective_id=number, has_side_effects=True
        )

    activated, slope, sums = pl.pallas_call(
        forward_kernel,
        out_shape=(
            jax.ShapeDtypeStruct((channels, count, cells), b16),
            jax.ShapeDtypeStruct((count, channels, cells), b16),
            jax.ShapeDtypeStruct((length, 128), b16),
        ),
        in_specs=[vmem] * 4,
        out_specs=(vmem,) * 3,
        scratch_shapes=[
            stack, tile, rows, edge, edge, patch, acc, rows,
            pltpu.VMEM((3 * channels, lanes * 128), f32),
            pltpu.SemaphoreType.DMA((4,)),
        ],
        compiler_params=params(0),
        cost_estimate=pl.CostEstimate(
            flops=2 * flops, bytes_accessed=4000000, transcendentals=0
        ),
    )(x, kernel_taps, bias_vector[None], cot)
    field_grad, kernel_grad, bias_row = pl.pallas_call(
        backward_kernel,
        out_shape=(
            jax.ShapeDtypeStruct((channels, count, cells), b16),
            jax.ShapeDtypeStruct((27, channels, channels), f32),
            jax.ShapeDtypeStruct((1, 128), f32),
        ),
        in_specs=[vmem] * 3,
        out_specs=(vmem,) * 3,
        scratch_shapes=[
            stack, tile, patch, acc, edge, edge,
            pltpu.VMEM((outer - 1, rows1, 128), b16),
            pltpu.VMEM((inner - 1, rows2, 128), b16),
            pltpu.VMEM((rows1, 128), b16),
            pltpu.VMEM((length, 128), b16),
            pltpu.SemaphoreType.DMA((4,)),
            pltpu.SemaphoreType.DMA((2 * (outer + inner),)),
            pltpu.SemaphoreType.DMA((2 * (outer + inner),)),
        ],
        compiler_params=params(1),
        cost_estimate=pl.CostEstimate(flops=flops, bytes_accessed=4000000, transcendentals=0),
    )(slope, kernel_taps, sums)
    return activated[None], field_grad[None], kernel_grad, bias_row[0, :channels]


def solution(mesh):
    in_specs = (
        P(("groups", "dp"), None, "gy", None),
        P(),
        P(),
        P(("groups", "dp"), None, "gy", None),
    )
    out_specs = (
        P(("groups", "dp"), None, "gy", None),
        P(("groups", "dp"), None, "gy", None),
        P("groups", None, None),
        P("groups"),
    )
    return jax.shard_map(shards, mesh=mesh, in_specs=in_specs, out_specs=out_specs, check_vma=False)
```
